128 devices in a mesh: fsdp: 64 (over x_lo, z, y, core), dp: 2 (over x_hi).
Axes of the slice: x: 4 (x_hi: 2, x_lo: 2; x = x_hi * 2 + x_lo), y: 4, z: 4, core: 2. Of those that a mesh axis runs over, the one named last changes fastest.
Arguments:
- queries: bfloat16 [256, 768], P(('fsdp', 'dp')), may hold values from -6 to 6
- w_proj: bfloat16 [768, 9216], P(None, 'fsdp'), may hold values from -0.21875 to 0.21875
- b_proj: bfloat16 [9216], P('fsdp'), may hold values from -3 to 3
- captions: bfloat16 [256, 9216], P(('fsdp', 'dp')), may hold values from -6 to 6
- ln_gain: float32 [9216], replicated, may hold values from 0.1 to 1.9
- ln_bias: float32 [9216], replicated, may hold values from -1.8 to 1.8
- fc1_weight: bfloat16 [9216, 36864], P(None, 'fsdp'), may hold values from -0.0625 to 0.0625
- fc1_bias: bfloat16 [36864], P('fsdp'), may hold values from -3 to 3
- fc2_weight: bfloat16 [36864, 9216], P('fsdp'), may hold values from -0.03125 to 0.03125
- fc2_bias: float32 [9216], replicated, may hold values from -1.8 to 1.8
- cotangent: bfloat16 [256, 9216], P(('fsdp', 'dp')), may hold values from -24 to 24
Outputs:
- out_queries: bfloat16 [256, 9216], P(('fsdp', 'dp'))
- out_captions: bfloat16 [256, 9216], P(('fsdp', 'dp'))
- grad_w_proj: float32 [768, 9216], P(None, 'fsdp')
- grad_b_proj: float32 [9216], P('fsdp')
The draws below stay inside these ranges and needn't reach their ends.
All inputs are finite; a program needn't handle non-finite values.
Results may differ from the reference program's by a relative error of at most 0.017.
The reference program's roundings to bfloat16 on the way (of `proj`, `act`, `hidden`, `grad_hidden` and `grad_input`) count: a program that leaves them out, or rounds other values in their place, can miss the bound.
Values may be sent and summed in bfloat16 or wider, within the bound.
No kernel may reach another device: no remote copies, remote signals or barrier semaphores. Data moves between devices by JAX's collectives and lax.ppermute only.
A program may use at most 192 MiB of HBM per device.

```python
import jax
import jax.numpy as jnp
from jax import lax

D = 9216
FF = 36864
QDIM = 768
TOKENS_Q = 256
TOKENS_C = 256


def with_spikes(entries, rng, source, target, parts, factor):
    owner, partner = [(jnp.arange(entries.shape[position]) // (entries.shape[position] // parts)).reshape([-1 if axis == position else 1 for axis in range(entries.ndim)]) for position in (source, target)]
    chosen = jax.random.permutation(rng, parts)[partner]
    strong = (owner == chosen) | (owner == (partner + parts // 2) % parts)
    return jnp.where(strong, factor * entries, entries)


def shard_levels(rng, shape, shards, smallest, high):
    factor_of = 1.0
    for position, shards_of in shards:
        steps = jax.random.uniform(jax.random.fold_in(jax.random.fold_in(rng, 6), position), (shards_of,), jnp.float32, smallest / len(shards), high / len(shards))
        factor_of = factor_of * jnp.repeat(jnp.exp(steps), shape[position] // shards_of).reshape((-1,) + (1,) * (len(shape) - 1 - position))
    return factor_of


def gaussian(own_key, shape, scale, bound, cuts=(), held_as=jnp.bfloat16):
    drawn = scale * jax.random.normal(own_key, shape, jnp.float32)
    if cuts:
        drawn = drawn * shard_levels(own_key, shape, cuts, -0.22, 0.18)
    return jnp.clip(drawn, -bound, bound).astype(held_as)


def heavy_noise(key, dims, scale, limit, shards, heavy, dtype=jnp.bfloat16):
    entries = scale * jax.random.normal(key, dims, jnp.float32)
    if shards:
        entries = entries * shard_levels(key, dims, shards, -0.22, 0.18)
    return jnp.clip(with_spikes(entries, jax.random.fold_in(key, 3), *heavy), -limit, limit).astype(dtype)


def setup_inputs(seed: int = 0) -> dict:
    keys = jax.random.split(jax.random.key(seed), 12)
    queries = gaussian(keys[0], (TOKENS_Q, QDIM), 1.0, 6.0, ((0, 128),))
    w_proj = gaussian(keys[1], (QDIM, D), QDIM ** -0.5, 0.21875, ((1, 64),))
    b_proj = gaussian(keys[2], (D,), 0.5, 3.0, ((0, 64),))
    captions = gaussian(keys[3], (TOKENS_C, D), 1.0, 6.0, ((0, 128),))
    ln_gain = jnp.clip(1.0 + 0.18 * jax.random.normal(keys[4], (D,), jnp.float32), 0.1, 1.9)
    ln_bias = gaussian(keys[5], (D,), 0.3, 1.8, (), jnp.float32)
    fc1_weight = gaussian(keys[6], (D, FF), D ** -0.5, 0.0625, ((1, 64),))
    fc1_bias = gaussian(keys[7], (FF,), 0.5, 3.0, ((0, 64),))
    fc2_weight = gaussian(keys[8], (FF, D), FF ** -0.5, 0.03125, ((0, 64),))
    fc2_bias = gaussian(keys[9], (D,), 0.3, 1.8, (), jnp.float32)
    cotangent = heavy_noise(keys[10], (TOKENS_Q, D), 1.0, 24.0, ((0, 128),), (0, 1, 128, 5.5))
    return dict(queries=queries, w_proj=w_proj, b_proj=b_proj, captions=captions, ln_gain=ln_gain, ln_bias=ln_bias, fc1_weight=fc1_weight, fc1_bias=fc1_bias, fc2_weight=fc2_weight, fc2_bias=fc2_bias, cotangent=cotangent)


def standardize(values):
    centre = lax.optimization_barrier(jnp.mean(values, axis=1, keepdims=True))
    shifted = values - centre
    inv_std = 1.0 / jnp.sqrt(lax.optimization_barrier(jnp.mean(shifted * shifted, axis=1, keepdims=True)) + 1e-05)
    return (shifted * inv_std, inv_std)

def forward_rows(values, ln_gain, ln_bias, fc1_weight, fc1_bias, fc2_weight, fc2_bias):
    normed, inv_std = standardize(values)
    act = (normed * ln_gain + ln_bias).astype(jnp.bfloat16)
    hidden = jnp.maximum(jnp.dot(act, fc1_weight, preferred_element_type=jnp.float32) + fc1_bias.astype(jnp.float32), 0.0).astype(jnp.bfloat16)
    output = values + jnp.dot(hidden, fc2_weight, preferred_element_type=jnp.float32) + fc2_bias
    return (output.astype(jnp.bfloat16), normed, inv_std, hidden)

def reference(queries, w_proj, b_proj, captions, ln_gain, ln_bias, fc1_weight, fc1_bias, fc2_weight, fc2_bias, cotangent):
    proj = (jnp.dot(queries, w_proj, preferred_element_type=jnp.float32) + b_proj.astype(jnp.float32)).astype(jnp.bfloat16)
    out_queries, normed, inv_std, hidden = forward_rows(proj.astype(jnp.float32), ln_gain, ln_bias, fc1_weight, fc1_bias, fc2_weight, fc2_bias)
    out_captions = forward_rows(captions.astype(jnp.float32), ln_gain, ln_bias, fc1_weight, fc1_bias, fc2_weight, fc2_bias)[0]
    back = jnp.dot(cotangent, fc2_weight.T, preferred_element_type=jnp.float32)
    grad_hidden = jnp.where(hidden > 0, back, 0.0).astype(jnp.bfloat16)
    grad_act = jnp.dot(grad_hidden, fc1_weight.T, preferred_element_type=jnp.float32)
    scaled = grad_act * ln_gain
    grad_input = cotangent.astype(jnp.float32) + inv_std * (scaled - lax.optimization_barrier(jnp.mean(scaled, axis=1, keepdims=True)) - normed * lax.optimization_barrier(jnp.mean(scaled * normed, axis=1, keepdims=True)))
    grad_input = grad_input.astype(jnp.bfloat16)
    grad_w_proj = jnp.dot(queries.T, grad_input, preferred_element_type=jnp.float32)
    grad_b_proj = lax.optimization_barrier(jnp.sum(grad_input.astype(jnp.float32), axis=0))
    return (out_queries, out_captions, grad_w_proj, grad_b_proj)
```

```python
import jax
import jax.numpy as jnp
from jax import lax
from jax.sharding import PartitionSpec as P

F32 = jnp.float32
BF16 = jnp.bfloat16
NX, NZ, NY, NC = 2, 4, 4, 2
LANES = 128


def pos(x, z, y, c):
    return ((x * NZ + z) * NY + y) * NC + c


def ring_pairs(along_z, shift):
    pairs = []
    for x in range(NX):
        for z in range(NZ):
            for y in range(NY):
                for c in range(NC):
                    if along_z[c]:
                        to = pos(x, (z + shift) % NZ, y, c)
                    else:
                        to = pos(x, z, (y + shift) % NY, c)
                    pairs.append((pos(x, z, y, c), to))
    return pairs


def swap_pairs(axis):
    pairs = []
    for x in range(NX):
        for z in range(NZ):
            for y in range(NY):
                for c in range(NC):
                    to = pos(1 - x, z, y, c) if axis == "x" else pos(x, z, y, 1 - c)
                    pairs.append((pos(x, z, y, c), to))
    return pairs


STAGE_A = (True, False)
STAGE_B = (False, True)


def send(value, pairs):
    return lax.ppermute(value, "fsdp", pairs)


def put(buffer, piece, index):
    return lax.dynamic_update_slice_in_dim(buffer, piece[None], index, 0)


def gather2(shard, axis, index):
    buffer = jnp.zeros((2,) + shard.shape, shard.dtype)
    buffer = put(buffer, shard, index)
    return put(buffer, send(shard, swap_pairs(axis)), 1 - index)


def gather4(shard, stage, index):
    got = [send(shard, ring_pairs(stage, k)) for k in (1, 2, 3)]
    buffer = jnp.zeros((4,) + shard.shape, shard.dtype)
    buffer = put(buffer, shard, index)
    for k in (1, 2, 3):
        buffer = put(buffer, got[k - 1], (index - k) % 4)
    return buffer


def take(blocks, index):
    return lax.dynamic_index_in_dim(blocks, index, 0, keepdims=False)


def scatter2(blocks, axis, index):
    got = send(take(blocks, 1 - index), swap_pairs(axis))
    return take(blocks, index).astype(F32) + got.astype(F32)


def scatter4(blocks, stage, index):
    got = [send(take(blocks, (index + k) % 4), ring_pairs(stage, k)) for k in (1, 2, 3)]
    total = take(blocks, index).astype(F32)
    for piece in got:
        total = total + piece.astype(F32)
    return total


def standardize(values):
    centre = jnp.mean(values, axis=1, keepdims=True)
    shifted = values - centre
    inv_std = 1.0 / jnp.sqrt(jnp.mean(shifted * shifted, axis=1, keepdims=True) + 1e-05)
    return shifted * inv_std, centre, inv_std


def split_hi_lo(value):
    hi = lax.reduce_precision(value, 8, 7)
    lo = lax.reduce_precision(value - hi, 8, 7)
    return hi.astype(BF16), lo.astype(BF16)


def body(
    queries,
    w_proj,
    b_proj,
    captions,
    ln_gain,
    ln_bias,
    fc1_weight,
    fc1_bias,
    fc2_weight,
    fc2_bias,
    cotangent,
):
    where = lax.axis_index("fsdp")
    c = where % NC
    y = (where // NC) % NY
    z = (where // (NC * NY)) % NZ
    x = where // (NC * NY * NZ)
    ia = jnp.where(c == 0, z, y)
    ib = jnp.where(c == 0, y, z)
    rows, width = captions.shape
    qdim = queries.shape[1]
    cols = w_proj.shape[1]
    group = NX * NZ * NY * NC
    tokens = group * rows
    half = tokens // 2
    near = 8 * rows

    nq, nw = rows * qdim // LANES, rows * width // LANES
    pack = jnp.concatenate(
        [queries.reshape(nq, LANES), captions.reshape(nw, LANES), cotangent.reshape(nw, LANES)], axis=0
    )
    pack = gather2(pack, "x", x)
    pack = gather4(pack, STAGE_A, ia).reshape(8, -1, LANES)
    q_near = pack[:, :nq].reshape(near, qdim)
    c_near = pack[:, nq : nq + nw].reshape(near, width)
    u_near = pack[:, nq + nw :].reshape(near, width)

    def far(value):
        value = gather4(value, STAGE_B, ib).reshape(half, -1)
        return gather2(value, "core", c).reshape(tokens, -1)

    query_all = far(q_near)
    other_query = lax.ppermute(query_all, "dp", [(0, 1), (1, 0)])
    proj_own = (
        lax.dot_general(w_proj, query_all, (((0,), (1,)), ((), ())), preferred_element_type=F32)
        + b_proj.astype(F32)[:, None]
    ).astype(BF16)
    caption_all = lax.optimization_barrier(far(c_near))
    upstream_all = lax.optimization_barrier(far(u_near))

    plane = gather2(proj_own, "x", x)
    plane = gather4(plane, STAGE_A, ia)
    plane = gather4(plane, STAGE_B, ib)
    both = gather2(plane, "core", c)
    plane0 = jnp.transpose(both[0], (2, 1, 0, 3, 4))
    plane1 = jnp.transpose(both[1], (2, 0, 1, 3, 4))
    proj_t = jnp.stack([plane0, plane1], axis=3).reshape(width, tokens)
    proj_all = lax.optimization_barrier(proj_t.T)

    gain_hi, gain_lo = split_hi_lo(ln_gain)
    bias_hi, bias_lo = split_hi_lo(ln_bias)
    normed_c = standardize(caption_all.astype(F32))[0]
    act_c = (normed_c * ln_gain + ln_bias).astype(BF16)
    extra = jnp.stack([gain_hi, gain_lo, bias_hi, bias_lo] + [jnp.zeros_like(gain_hi)] * 12)
    pre_c = jnp.dot(jnp.concatenate([act_c, extra], axis=0), fc1_weight, preferred_element_type=F32)
    gain_w = pre_c[tokens] + pre_c[tokens + 1]
    bias_w = pre_c[tokens + 2] + pre_c[tokens + 3]
    b1 = fc1_bias.astype(F32)
    hidden_c = jnp.maximum(pre_c[:tokens] + b1, 0.0).astype(BF16)
    part_c = jnp.dot(hidden_c, fc2_weight, preferred_element_type=F32).astype(BF16)

    back = lax.dot_general(
        upstream_all, fc2_weight, (((1,), (1,)), ((), ())), preferred_element_type=F32
    )
    normed_q, centre, inv_std = standardize(proj_all.astype(F32))
    act_q = (normed_q * ln_gain + ln_bias).astype(BF16)
    pre_q = jnp.dot(act_q, fc1_weight, preferred_element_type=F32)
    hidden_q = jnp.maximum(pre_q + b1, 0.0).astype(BF16)
    grad_hidden = jnp.where(hidden_q > 0, back, 0.0).astype(BF16)
    part_g = lax.dot_general(
        fc1_weight, grad_hidden, (((1,), (1,)), ((), ())), preferred_element_type=F32
    ).astype(BF16)
    part_q = jnp.dot(hidden_q, fc2_weight, preferred_element_type=F32).astype(BF16)

    gh = grad_hidden.astype(F32)
    mean1 = jnp.sum(gh * gain_w, axis=1) / width
    mean2 = jnp.sum(gh * (pre_q - bias_w), axis=1) / width

    def with_stats(blocks, stats):
        s1, s2 = stats
        rows_of = [*split_hi_lo(s1), *split_hi_lo(s2)] + [jnp.zeros((tokens,), BF16)] * 12
        tail = jnp.stack(rows_of)
        tail = jnp.broadcast_to(tail, (blocks.shape[0],) + tail.shape)
        return jnp.concatenate([blocks.reshape(blocks.shape[0], -1, tokens), tail], axis=1)

    def unpack(total):
        tail = total[-16:]
        return total[:-16].astype(BF16), (tail[0] + tail[1], tail[2] + tail[3])

    grid = part_g.reshape(NX, NZ, NY, NC, cols, tokens)
    plane0 = jnp.transpose(grid[:, :, :, 0], (2, 1, 0, 3, 4)).reshape(-1, tokens)
    plane1 = jnp.transpose(grid[:, :, :, 1], (1, 2, 0, 3, 4)).reshape(-1, tokens)
    blocks = jnp.stack([plane0, plane1])
    part, stats = unpack(scatter2(with_stats(blocks, (mean1, mean2)), "core", c))
    part, stats = unpack(scatter4(with_stats(part.reshape(4, -1, tokens), stats), STAGE_B, ib))
    part, stats = unpack(scatter4(with_stats(part.reshape(4, -1, tokens), stats), STAGE_A, ia))
    total = scatter2(with_stats(part.reshape(2, -1, tokens), stats), "x", x)
    grad_act, tail = total[:cols], total[cols:]
    mean1, mean2 = tail[0] + tail[1], tail[2] + tail[3]

    def scatter_rows(part):
        part = scatter2(part.reshape(2, half, width), "core", c).astype(BF16)
        part = scatter4(part.reshape(4, near, width), STAGE_B, ib).astype(BF16)
        part = scatter4(part.reshape(4, 2 * nw, LANES), STAGE_A, ia).astype(BF16)
        part = scatter2(part.reshape(2, nw, LANES), "x", x)
        return part.reshape(rows, width)

    out_captions = (captions.astype(F32) + scatter_rows(part_c) + fc2_bias).astype(BF16)
    first = c * half + (ib * 8 + ia * 2 + x) * rows
    own = lax.dynamic_slice_in_dim(proj_all, first, rows, 0)
    out_queries = (own.astype(F32) + scatter_rows(part_q) + fc2_bias).astype(BF16)

    gain_own = lax.dynamic_slice_in_dim(ln_gain, where * cols, cols, 0)[:, None]
    cot_own = lax.dynamic_slice_in_dim(upstream_all, where * cols, cols, 1).astype(F32).T
    inv_row = inv_std.reshape(1, tokens)
    normed_own = (proj_own.astype(F32) - centre.reshape(1, tokens)) * inv_row
    scaled = grad_act * gain_own
    grad_input = (
        cot_own + inv_row * (scaled - mean1[None, :] - normed_own * mean2[None, :])
    ).astype(BF16)
    other_input = lax.ppermute(grad_input, "dp", [(0, 1), (1, 0)])

    def terms(query_rows, grads):
        weight = lax.dot_general(
            query_rows, grads, (((0,), (1,)), ((), ())), preferred_element_type=F32
        )
        return weight, jnp.sum(grads.astype(F32), axis=1)

    weight0, bias0 = terms(query_all, grad_input)
    weight1, bias1 = terms(other_query, other_input)
    return out_queries, out_captions, weight0 + weight1, bias0 + bias1


def solution(mesh):
    placed = (
        P(("fsdp", "dp"), None),
        P(None, "fsdp"),
        P("fsdp"),
        P(("fsdp", "dp"), None),
        P(),
        P(),
        P(None, "fsdp"),
        P("fsdp"),
        P("fsdp", None),
        P(),
        P(("fsdp", "dp"), None),
    )
    return jax.shard_map(
        body,
        mesh=mesh,
        in_specs=placed,
        out_specs=(P(("fsdp", "dp"), None), P(("fsdp", "dp"), None), P(None, "fsdp"), P("fsdp")),
        check_vma=False,
    )
```

```python
import jax
import jax.numpy as jnp
from jax import lax
from jax.experimental import pallas as pl
from jax.experimental.pallas import tpu as pltpu
from jax.sharding import PartitionSpec as P

F32 = jnp.float32
BF16 = jnp.bfloat16
NX, NZ, NY, NC = 2, 4, 4, 2
LANES = 128


def pos(x, z, y, c):
    return ((x * NZ + z) * NY + y) * NC + c


def ring_pairs(along_z, shift):
    pairs = []
    for x in range(NX):
        for z in range(NZ):
            for y in range(NY):
                for c in range(NC):
                    if along_z[c]:
                        to = pos(x, (z + shift) % NZ, y, c)
                    else:
                        to = pos(x, z, (y + shift) % NY, c)
                    pairs.append((pos(x, z, y, c), to))
    return pairs


def swap_pairs(axis):
    pairs = []
    for x in range(NX):
        for z in range(NZ):
            for y in range(NY):
                for c in range(NC):
                    to = pos(1 - x, z, y, c) if axis == "x" else pos(x, z, y, 1 - c)
                    pairs.append((pos(x, z, y, c), to))
    return pairs


STAGE_A = (True, False)
STAGE_B = (False, True)


def send(value, pairs):
    return lax.ppermute(value, "fsdp", pairs)


def put(buffer, piece, index):
    return lax.dynamic_update_slice_in_dim(buffer, piece[None], index, 0)


def gather2(shard, axis, index):
    buffer = jnp.zeros((2,) + shard.shape, shard.dtype)
    buffer = put(buffer, shard, index)
    return put(buffer, send(shard, swap_pairs(axis)), 1 - index)


def gather4(shard, stage, index):
    got = [send(shard, ring_pairs(stage, k)) for k in (1, 2, 3)]
    buffer = jnp.zeros((4,) + shard.shape, shard.dtype)
    buffer = put(buffer, shard, index)
    for k in (1, 2, 3):
        buffer = put(buffer, got[k - 1], (index - k) % 4)
    return buffer


def take(blocks, index):
    return lax.dynamic_index_in_dim(blocks, index, 0, keepdims=False)


def scatter2(blocks, axis, index):
    got = send(take(blocks, 1 - index), swap_pairs(axis))
    return take(blocks, index).astype(F32) + got.astype(F32)


def scatter4(blocks, stage, index):
    got = [send(take(blocks, (index + k) % 4), ring_pairs(stage, k)) for k in (1, 2, 3)]
    total = take(blocks, index).astype(F32)
    for piece in got:
        total = total + piece.astype(F32)
    return total


CHUNK = 3072
PIECE = 16
SENT = [(0, 1), (1, 0)]


def row_stats(ref, width):
    rows = ref.shape[0]
    step = width // 8

    def total(of):
        def add(i, acc):
            for j in range(step // LANES):
                acc = acc + of(ref[:, pl.ds(pl.multiple_of(i * step, LANES) + j * LANES, LANES)].astype(F32))
            return acc

        acc = lax.fori_loop(0, 8, add, jnp.zeros((rows, LANES), F32))
        return jnp.sum(acc, axis=1, keepdims=True) / width

    centre = total(lambda v: v)
    inv_std = 1.0 / jnp.sqrt(total(lambda v: (v - centre) * (v - centre)) + 1e-05)
    return centre, inv_std


def chunk_of(i):
    return pl.ds(pl.multiple_of(i * CHUNK, CHUNK), CHUNK)


def at_piece(i):
    return pl.ds(pl.multiple_of(i * PIECE, PIECE), PIECE)


def own_rows(place, value):
    first = (place[1] * 2 + place[3]) * 2
    row = lax.broadcasted_iota(jnp.int32, value.shape, 0)
    return jnp.where((row == first) | (row == first + 1), value, 0.0)


def columns_copy(source, target, sems, i):
    cols = chunk_of(i)
    return pltpu.make_async_copy(source.at[:, cols], target.at[:, cols], sems.at[i])


def each_chunk(width, step):
    def run(i, carry):
        step(i, chunk_of(i))
        return carry

    lax.fori_loop(0, width // CHUNK, run, 0)


def token_block(place, i):
    c, ia, ib = place[0], place[1], place[2]
    k = i % 4
    if i < 4:
        return c * 4 + lax.rem(ib - k + 4, 4)
    return (1 - c) * 4 + lax.rem(ia - k + 4, 4)


NT = (((1,), (1,)), ((), ()))


def early_kernel(place, *refs):
    pieces, refs = refs[:2], refs[2:]
    (w2, gain, bias), refs = refs[:3], refs[3:]
    act, back, cot_own, cap, cot, back_t, w2v, sem, sem2 = refs
    width = cap.shape[1]
    lead = pieces[0].shape[1] - 2 * width
    copies = []
    for i in range(8):
        rows = pl.ds(i % 4 * PIECE, PIECE)
        near_rows = pieces[i // 4].at[rows, pl.ds(lead, width)]
        copies.append(pltpu.make_async_copy(near_rows, cap.at[pl.ds(i * PIECE, PIECE)], sem.at[i]))
    for copy in copies:
        copy.start()
    each_chunk(width, lambda i, cols: columns_copy(w2, w2v, sem2, i).start())
    for i in range(8):
        rows = pl.ds(i % 4 * PIECE, PIECE)
        near_rows = pieces[i // 4].at[rows, pl.ds(lead + width, width)]
        spot = at_piece(token_block(place, i))
        copies.append(pltpu.make_async_copy(near_rows, cot.at[spot], sem.at[8 + i]))
        copies[-1].start()
    for copy in copies[:8]:
        copy.wait()
    centre, inv_std = row_stats(cap, width)
    back_t[...] = jnp.zeros_like(back_t)
    for copy in copies[8:]:
        copy.wait()

    def step(i, cols):
        normed = (cap[:, cols].astype(F32) - centre) * inv_std
        act[:, cols] = (normed * gain[:, cols] + bias[:, cols]).astype(BF16)
        columns_copy(w2, w2v, sem2, i).wait()
        back_t[...] += lax.dot_general(w2v[:, cols], cot[:, cols], NT, preferred_element_type=F32)

    each_chunk(width, step)
    back[...] = back_t[...].T
    size = cot_own.shape[0]
    start = place[4] * size
    aligned = pl.multiple_of(start // LANES * LANES, LANES)
    near = cot[:, pl.ds(aligned, 2 * LANES)].astype(F32)
    near = pltpu.roll(near, lax.rem(2 * LANES - lax.rem(start, LANES), 2 * LANES), 1)
    cot_own[...] = near.T[:size]


def main_kernel(place, *refs):
    pieces, refs = refs[:2], refs[2:]
    (caps, act_c, back, w1, w2, gain, bias, b1, b2), refs = refs[:9], refs[9:]
    (kept, kept_far, sent, sent_far, stats), refs = refs[:5], refs[5:]
    proj_t, proj, acc, order, hidden, own_c, w1v, w2v, sem, sem1, sem2 = refs
    grad_t = proj_t
    width = proj.shape[1]
    tokens = proj.shape[0]
    size = width // 64
    c, ia, ib = place[0], place[1], place[2]

    def block_of(half, k, j, other_x):
        if half == 0:
            core, a, b = c, lax.rem(ia - j + 4, 4), lax.rem(ib - k + 4, 4)
        else:
            core, a, b = 1 - c, lax.rem(ib - j + 4, 4), lax.rem(ia - k + 4, 4)
        x = place[3] + other_x - 2 * place[3] * other_x
        z_y = jnp.where(core == 0, a * 8 + b * 2, b * 8 + a * 2)
        return pl.ds(pl.multiple_of((x * 32 + z_y + core) * size, PIECE), size)

    lead = caps.shape[1] - 2 * width
    own_rows_copy = pltpu.make_async_copy(caps.at[pl.ds(0, PIECE), pl.ds(lead, width)], own_c, sem.at[0])
    own_rows_copy.start()
    each_chunk(width, lambda i, cols: columns_copy(w1, w1v, sem1, i).start())
    for half in (0, 1):

        def bring_block(n, carry):
            source = pl.ds(pl.multiple_of(n * size, PIECE), size)
            proj_t[block_of(half, n // 8, n // 2 % 4, n % 2)] = pieces[half][source]
            return carry

        lax.fori_loop(0, 32, bring_block, 0, unroll=8)

    def turn(i, cols):
        proj[:, cols] = proj_t[cols].T

    each_chunk(width, turn)
    centre, inv_std = row_stats(proj, width)
    acc[...] = jnp.zeros_like(acc)

    def first(i, cols):
        normed = (proj[:, cols].astype(F32) - centre) * inv_std
        act = (normed * gain[:, cols] + bias[:, cols]).astype(BF16)
        act = jnp.concatenate([act_c[:, cols], act], axis=0)
        columns_copy(w1, w1v, sem1, i).wait()
        columns_copy(w2, w2v, sem2, i).start()
        acc[...] += lax.dot_general(w1v[:, cols], act, NT, preferred_element_type=F32)

    each_chunk(width, first)
    order[...] = jnp.maximum(acc[...].T + b1[...], 0.0).astype(BF16)
    grad_hidden = jnp.where(order[tokens:].astype(F32) > 0, back[...], 0.0).astype(BF16)

    def gradient(i, carry):
        cols = chunk_of(i)
        value = jnp.dot(grad_hidden, w1v[:, cols], preferred_element_type=F32)
        grad_t[cols] = value.astype(BF16).T
        normed = (proj[:, cols].astype(F32) - centre) * inv_std
        scaled = value * gain[:, cols]
        both = scaled * normed
        sum1, sum2 = carry
        for k in range(CHUNK // LANES):
            lanes = slice(k * LANES, (k + 1) * LANES)
            sum1, sum2 = sum1 + scaled[:, lanes], sum2 + both[:, lanes]
        return sum1, sum2

    zero = jnp.zeros((tokens, LANES), F32)
    sum1, sum2 = lax.fori_loop(0, width // CHUNK, gradient, (zero, zero))
    square = (tokens, tokens)

    def as_row(column):
        return jnp.broadcast_to(column, square).T[0:1]

    mean1 = as_row(jnp.sum(sum1, axis=1, keepdims=True) / width)
    mean2 = as_row(jnp.sum(sum2, axis=1, keepdims=True) / width)
    row = lax.broadcasted_iota(jnp.int32, (PIECE, tokens), 0)
    tail = jnp.where(row == 0, mean1, jnp.where(row == 1, mean2, 0.0)).astype(BF16)
    stats[...] = jnp.where(row < 8, as_row(centre), as_row(inv_std))
    tile_rows = 2 * PIECE
    grad_rows = 8 * (size + PIECE)
    piece_rows = grad_rows + width // LANES * tile_rows
    for half, first_k, out in ((1, 0, sent), (1, 1, sent_far), (0, 0, kept), (0, 1, kept_far)):

        def place_block(n, carry):
            k = n // 8
            base = pl.multiple_of(k * piece_rows + n % 8 * (size + PIECE), PIECE)
            out[pl.ds(base, size)] = grad_t[block_of(half, k + first_k, n // 2 % 4, n % 2)]
            out[pl.ds(base + size, PIECE)] = tail
            return carry

        lax.fori_loop(0, 24 if first_k else 8, place_block, 0, unroll=8)
    for i in range(8):
        base = 2 * i * PIECE
        hidden[base : base + PIECE] = order[i * PIECE : (i + 1) * PIECE]
        block = token_block(place, i)
        hidden[base + PIECE : base + 2 * PIECE] = order[at_piece(tokens // PIECE + block)]
    mine = at_piece(token_block(place, 0))
    own_rows_copy.wait()

    def second(i, cols):
        columns_copy(w2, w2v, sem2, i).wait()
        value = jnp.dot(hidden[...], w2v[:, cols], preferred_element_type=F32)
        first_c = value[:PIECE] + own_rows(place, own_c[:, cols].astype(F32) + b2[:, cols])
        first_q = value[PIECE : 2 * PIECE] + own_rows(place, proj[mine, cols].astype(F32) + b2[:, cols])
        value = jnp.concatenate([first_c, first_q, value[2 * PIECE :]], axis=0).astype(BF16)
        tiles = CHUNK // LANES
        for k in range(8):
            out = (kept, kept_far, sent, sent_far)[k // 4 * 2 + (k % 4 > 0)]
            base = max(k % 4 - 1, 0) * piece_rows + grad_rows + i * tiles * tile_rows
            for j in range(tiles):
                spot = pl.ds(pl.multiple_of(base + j * tile_rows, tile_rows), tile_rows)
                out[spot] = value[k * tile_rows : (k + 1) * tile_rows, j * LANES : (j + 1) * LANES]

    each_chunk(width, second)


def middle_kernel(place, *refs):
    sums, (own, *away), total = refs[:5], refs[6:10], refs[10]
    grad_rows = own.shape[1] // 14 * 5 * 8
    total[...] = sum(ref[grad_rows:].astype(F32) for ref in sums)
    ia, here = place[1], place[3]
    size = own.shape[1] // 14 * 5
    half = (own.shape[1] - size) // 2
    tile_rows = 2 * PIECE
    for j in range(4):
        out = own if j == 0 else away[j - 1]
        for other_x in range(2):
            a = lax.rem(ia - j + 4, 4)
            x = here + other_x - 2 * here * other_x
            spot = slice((j * 2 + other_x) * size, (j * 2 + other_x + 1) * size)
            out[other_x, :size] = sum(ref[spot].astype(F32) for ref in sums).astype(out.dtype)
            for kind in range(2):
                token = kind * PIECE + a * 4 + x * 2
                rows = [
                    total[pl.ds(token + r, half // 2, stride=tile_rows)] for r in range(2)
                ]
                base = size + kind * half
                out[other_x, base : base + half] = jnp.concatenate(rows, axis=0).astype(out.dtype)


ANY = pl.BlockSpec(memory_space=pl.ANY)
VMEM = pl.BlockSpec(memory_space=pltpu.VMEM)
SMEM = pl.BlockSpec(memory_space=pltpu.SMEM)


def call(kernel, ins, outs, scratch, limit, micros):
    return pl.pallas_call(
        kernel,
        in_specs=[spec for spec, _ in ins],
        out_specs=[spec for spec, _, _ in outs],
        out_shape=[jax.ShapeDtypeStruct(shape, dtype) for _, shape, dtype in outs],
        scratch_shapes=scratch,
        compiler_params=pltpu.CompilerParams(vmem_limit_bytes=limit * 1024 * 1024),
        cost_estimate=pl.CostEstimate(flops=0, bytes_accessed=micros * 3_690_000, transcendentals=0),
    )(*[value for _, value in ins])


def body(
    queries,
    w_proj,
    b_proj,
    captions,
    ln_gain,
    ln_bias,
    fc1_weight,
    fc1_bias,
    fc2_weight,
    fc2_bias,
    cotangent,
):
    where = lax.axis_index("fsdp")
    c = where % NC
    y = (where // NC) % NY
    z = (where // (NC * NY)) % NZ
    x = where // (NC * NY * NZ)
    ia = jnp.where(c == 0, z, y)
    ib = jnp.where(c == 0, y, z)
    place = jnp.stack([c, ia, ib, x, where]).astype(jnp.int32)
    rows, width = captions.shape
    qdim = queries.shape[1]
    cols = w_proj.shape[1]
    units = fc1_weight.shape[1]
    group = NX * NZ * NY * NC
    tokens = group * rows
    half = tokens // 2
    near = 8 * rows
    nw = rows * width // LANES

    def around(value, stage):
        return [value, *lax.optimization_barrier([send(value, ring_pairs(stage, k)) for k in (1, 2, 3)])]

    pack = jnp.concatenate([queries, captions, cotangent], axis=1)
    pack = gather2(pack, "x", x)
    pack = gather4(pack, STAGE_A, ia).reshape(near, -1)


    query_half = gather4(pack[:, :qdim], STAGE_B, ib).reshape(half, qdim)
    query_all = gather2(query_half, "core", c).reshape(tokens, qdim)
    other_query = lax.ppermute(query_all, "dp", SENT)
    proj_own = (
        lax.dot_general(w_proj, query_all, (((0,), (1,)), ((), ())), preferred_element_type=F32)
        + b_proj.astype(F32)[:, None]
    ).astype(BF16)
    pack = pack[:, qdim:]
    pack_pieces = [pack] + [send(pack, ring_pairs(STAGE_B, k)) for k in (1, 2)]

    pair = jnp.concatenate([proj_own, send(proj_own, swap_pairs("x"))], axis=0)
    plane = jnp.concatenate(around(pair, STAGE_A), axis=0)
    plane, pack = lax.optimization_barrier((plane, pack))
    pack_pieces.append(send(pack, ring_pairs(STAGE_B, 3)))
    planes = []
    for pieces in (pack_pieces, around(plane, STAGE_B)):
        own_plane = jnp.concatenate(pieces, axis=0)
        planes.append([own_plane, send(own_plane, swap_pairs("core"))])
    pack_planes, proj_planes = planes
    scratch = pltpu.VMEM
    dma = pltpu.SemaphoreType.DMA

    gain, bias = ln_gain[None, :], ln_bias[None, :]
    b1, b2 = fc1_bias.astype(F32)[None, :], fc2_bias[None, :]
    w1_t = fc1_weight.T
    size = cols + PIECE

    act_c, back, cot_own = call(
        early_kernel,
        [(SMEM, place)]
        + [(ANY, piece) for piece in pack_planes]
        + [(ANY, fc2_weight), (VMEM, gain), (VMEM, bias)],
        [(VMEM, (tokens, width), BF16), (VMEM, (tokens, units), F32), (VMEM, (cols, tokens), F32)],
        [
            scratch((tokens, width), BF16),
            scratch((tokens, width), BF16),
            scratch((units, tokens), F32),
            scratch((units, width), BF16),
            dma((16,)),
            dma((width // CHUNK,)),
        ],
        50,
        10,
    )

    grad_rows, out_rows = 8 * size, width // LANES * 2 * PIECE
    piece_rows = grad_rows + out_rows
    kept, kept_far, sent, sent_far, stats = call(
        main_kernel,
        [(SMEM, place)]
        + [(VMEM, piece) for piece in proj_planes]
        + [(ANY, pack_planes[0]), (VMEM, act_c), (VMEM, back), (ANY, w1_t), (ANY, fc2_weight)]
        + [(VMEM, gain), (VMEM, bias), (VMEM, b1), (VMEM, b2)],
        [(VMEM, (piece_rows, LANES), BF16), (VMEM, (3 * piece_rows, LANES), BF16)] * 2
        + [(VMEM, (PIECE, tokens), F32)],
        [
            scratch((width, tokens), BF16),
            scratch((tokens, width), BF16),
            scratch((units, 2 * tokens), F32),
            scratch((2 * tokens, units), BF16),
            scratch((2 * tokens, units), BF16),
            scratch((PIECE, width), BF16),
            scratch((units, width), BF16),
            scratch((units, width), BF16),
            dma((1,)),
            dma((width // CHUNK,)),
            dma((width // CHUNK,)),
        ],
        42,
        20,
    )

    total = (kept_far.astype(F32) + send(sent_far, swap_pairs("core")).astype(F32)).astype(BF16)
    got = [send(part, ring_pairs(STAGE_B, -1 - k)) for k, part in enumerate(total.reshape(3, piece_rows, LANES))]
    last = size + 2 * nw
    own, *away = call(
        middle_kernel,
        [(SMEM, place), (VMEM, kept), (VMEM, send(sent, swap_pairs("core")))]
        + [(VMEM, part) for part in got]
        + [(ANY, other_query)],
        [(VMEM, (2, last, LANES), F32)] + [(VMEM, (2, last, LANES), BF16)] * 3,
        [scratch((out_rows, LANES), F32)],
        16,
        3,
    )
    got = lax.optimization_barrier([send(away[k - 1], ring_pairs(STAGE_A, -k)) for k in (1, 2, 3)])
    total = own + sum(part.astype(F32) for part in got)
    total = total[0] + send(total[1].astype(BF16), swap_pairs("x")).astype(F32)
    grad_act, mean1, mean2 = total[:cols], total[cols : cols + 1], total[cols + 1 : cols + 2]
    part = lax.optimization_barrier(total[size:].astype(BF16))
    out_captions, out_queries = part[:nw].reshape(rows, width), part[nw:].reshape(rows, width)

    gain_own = lax.dynamic_slice_in_dim(ln_gain, where * cols, cols, 0)[:, None]
    centre, inv_std = stats[0:1], stats[8:9]
    normed_own = (proj_own.astype(F32) - centre) * inv_std
    scaled = grad_act * gain_own
    grad_input = (cot_own + inv_std * (scaled - mean1 - normed_own * mean2)).astype(BF16)
    other_input = lax.ppermute(grad_input, "dp", SENT)

    def terms(query_rows, grads):
        weight = lax.dot_general(
            query_rows, grads, (((0,), (1,)), ((), ())), preferred_element_type=F32
        )
        return weight, jnp.sum(grads.astype(F32), axis=1)

    weight0, bias0 = terms(query_all, grad_input)
    weight1, bias1 = terms(other_query, other_input)
    return out_queries, out_captions, weight0 + weight1, bias0 + bias1


def solution(mesh):
    placed = (
        P(("fsdp", "dp"), None),
        P(None, "fsdp"),
        P("fsdp"),
        P(("fsdp", "dp"), None),
        P(),
        P(),
        P(None, "fsdp"),
        P("fsdp"),
        P("fsdp", None),
        P(),
        P(("fsdp", "dp"), None),
    )
    return jax.shard_map(
        body,
        mesh=mesh,
        in_specs=placed,
        out_specs=(P(("fsdp", "dp"), None), P(("fsdp", "dp"), None), P(None, "fsdp"), P("fsdp")),
        check_vma=False,
    )
```

```python
import jax
import jax.numpy as jnp
from jax import lax
from jax.experimental import pallas as pl
from jax.experimental.pallas import tpu as pltpu
from jax.sharding import PartitionSpec as P

F32 = jnp.float32
BF16 = jnp.bfloat16
NX, NZ, NY, NC = 2, 4, 4, 2
LANES = 128


def pos(x, z, y, c):
    return ((x * NZ + z) * NY + y) * NC + c


def ring_pairs(along_z, shift):
    pairs = []
    for x in range(NX):
        for z in range(NZ):
            for y in range(NY):
                for c in range(NC):
                    if along_z[c]:
                        to = pos(x, (z + shift) % NZ, y, c)
                    else:
                        to = pos(x, z, (y + shift) % NY, c)
                    pairs.append((pos(x, z, y, c), to))
    return pairs


def swap_pairs(axis):
    pairs = []
    for x in range(NX):
        for z in range(NZ):
            for y in range(NY):
                for c in range(NC):
                    to = pos(1 - x, z, y, c) if axis == "x" else pos(x, z, y, 1 - c)
                    pairs.append((pos(x, z, y, c), to))
    return pairs


STAGE_A = (True, False)
STAGE_B = (False, True)


def send(value, pairs):
    return lax.ppermute(value, "fsdp", pairs)


def put(buffer, piece, index):
    return lax.dynamic_update_slice_in_dim(buffer, piece[None], index, 0)


def gather2(shard, axis, index):
    buffer = jnp.zeros((2,) + shard.shape, shard.dtype)
    buffer = put(buffer, shard, index)
    return put(buffer, send(shard, swap_pairs(axis)), 1 - index)


def gather4(shard, stage, index):
    got = [send(shard, ring_pairs(stage, k)) for k in (1, 2, 3)]
    buffer = jnp.zeros((4,) + shard.shape, shard.dtype)
    buffer = put(buffer, shard, index)
    for k in (1, 2, 3):
        buffer = put(buffer, got[k - 1], (index - k) % 4)
    return buffer


def take(blocks, index):
    return lax.dynamic_index_in_dim(blocks, index, 0, keepdims=False)


def scatter2(blocks, axis, index):
    got = send(take(blocks, 1 - index), swap_pairs(axis))
    return take(blocks, index).astype(F32) + got.astype(F32)


def scatter4(blocks, stage, index):
    got = [send(take(blocks, (index + k) % 4), ring_pairs(stage, k)) for k in (1, 2, 3)]
    total = take(blocks, index).astype(F32)
    for piece in got:
        total = total + piece.astype(F32)
    return total


CHUNK = 3072
PIECE = 16
SENT = [(0, 1), (1, 0)]


def row_stats(ref, width):
    rows = ref.shape[0]
    step = width // 8

    def total(of):
        def add(i, acc):
            for j in range(step // LANES):
                acc = acc + of(ref[:, pl.ds(pl.multiple_of(i * step, LANES) + j * LANES, LANES)].astype(F32))
            return acc

        acc = lax.fori_loop(0, 8, add, jnp.zeros((rows, LANES), F32))
        return jnp.sum(acc, axis=1, keepdims=True) / width

    centre = total(lambda v: v)
    inv_std = 1.0 / jnp.sqrt(total(lambda v: (v - centre) * (v - centre)) + 1e-05)
    return centre, inv_std


def chunk_of(i):
    return pl.ds(pl.multiple_of(i * CHUNK, CHUNK), CHUNK)


def at_piece(i):
    return pl.ds(pl.multiple_of(i * PIECE, PIECE), PIECE)


def own_rows(place, value):
    first = (place[1] * 2 + place[3]) * 2
    row = lax.broadcasted_iota(jnp.int32, value.shape, 0)
    return jnp.where((row == first) | (row == first + 1), value, 0.0)


def columns_copy(source, target, sems, i):
    cols = chunk_of(i)
    return pltpu.make_async_copy(source.at[:, cols], target.at[:, cols], sems.at[i])


def each_chunk(width, step):
    def run(i, carry):
        step(i, chunk_of(i))
        return carry

    lax.fori_loop(0, width // CHUNK, run, 0)


def token_block(place, i):
    c, ia, ib = place[0], place[1], place[2]
    k = i % 4
    if i < 4:
        return c * 4 + lax.rem(ib - k + 4, 4)
    return (1 - c) * 4 + lax.rem(ia - k + 4, 4)


NT = (((1,), (1,)), ((), ()))


def early_kernel(place, *refs):
    pieces, refs = refs[:8], refs[8:]
    gain, bias, act, cot, cot_own, own, cap, sem = refs
    width = cap.shape[1]
    lead = pieces[0].shape[1] - 2 * width
    copies = []
    for i in range(8):
        near_rows = pieces[i].at[:, pl.ds(lead, width)]
        copies.append(pltpu.make_async_copy(near_rows, cap.at[pl.ds(i * PIECE, PIECE)], sem.at[i]))
    for copy in copies:
        copy.start()
    for i in range(8):
        near_rows = pieces[i].at[:, pl.ds(lead + width, width)]
        spot = at_piece(token_block(place, i))
        copies.append(pltpu.make_async_copy(near_rows, cot.at[spot], sem.at[8 + i]))
        copies[-1].start()
    for copy in copies[:8]:
        copy.wait()
    own[...] = cap[:PIECE]
    centre, inv_std = row_stats(cap, width)

    def step(i, cols):
        normed = (cap[:, cols].astype(F32) - centre) * inv_std
        act[:, cols] = (normed * gain[:, cols] + bias[:, cols]).astype(BF16)

    each_chunk(width, step)
    for copy in copies[8:]:
        copy.wait()
    size = cot_own.shape[0]
    start = place[4] * size
    aligned = pl.multiple_of(start // LANES * LANES, LANES)
    near = cot[:, pl.ds(aligned, 2 * LANES)].astype(F32)
    near = pltpu.roll(near, lax.rem(2 * LANES - lax.rem(start, LANES), 2 * LANES), 1)
    cot_own[...] = near.T[:size]


def main_kernel(place, *refs):
    pieces, refs = refs[:8], refs[8:]
    (own_c, act_c, cot, w1, w2, gain, bias, b1, b2), refs = refs[:9], refs[9:]
    outs, stats, refs = refs[:8], refs[8], refs[9:]
    proj_t, proj, acc, back_t, order, hidden, w1v, w2v, sem1, sem2 = refs
    grad_t = proj_t
    width = proj.shape[1]
    tokens = proj.shape[0]
    size = width // 64
    c, ia, ib = place[0], place[1], place[2]

    def block_of(half, k, j, other_x):
        if half == 0:
            core, a, b = c, lax.rem(ia - j + 4, 4), lax.rem(ib - k + 4, 4)
        else:
            core, a, b = 1 - c, lax.rem(ib - j + 4, 4), lax.rem(ia - k + 4, 4)
        x = place[3] + other_x - 2 * place[3] * other_x
        z_y = jnp.where(core == 0, a * 8 + b * 2, b * 8 + a * 2)
        return pl.ds(pl.multiple_of((x * 32 + z_y + core) * size, PIECE), size)

    each_chunk(width, lambda i, cols: columns_copy(w1, w1v, sem1, i).start())
    for i in range(8):

        def bring_block(n, carry):
            source = pl.ds(pl.multiple_of(n * size, PIECE), size)
            proj_t[block_of(i // 4, i % 4, n // 2, n % 2)] = pieces[i][source]
            return carry

        lax.fori_loop(0, 8, bring_block, 0, unroll=8)

    def turn(i, cols):
        proj[:, cols] = proj_t[cols].T

    each_chunk(width, turn)
    centre, inv_std = row_stats(proj, width)
    acc[...] = jnp.zeros_like(acc)

    def first(i, cols):
        normed = (proj[:, cols].astype(F32) - centre) * inv_std
        act = (normed * gain[:, cols] + bias[:, cols]).astype(BF16)
        act = jnp.concatenate([act_c[:, cols], act], axis=0)
        columns_copy(w1, w1v, sem1, i).wait()
        columns_copy(w2, w2v, sem2, i).start()
        acc[...] += lax.dot_general(w1v[:, cols], act, NT, preferred_element_type=F32)

    each_chunk(width, first)
    order[...] = jnp.maximum(acc[...].T + b1[...], 0.0).astype(BF16)
    back_t[...] = jnp.zeros_like(back_t)

    def backward(i, cols):
        columns_copy(w2, w2v, sem2, i).wait()
        back_t[...] += lax.dot_general(w2v[:, cols], cot[:, cols], NT, preferred_element_type=F32)

    each_chunk(width, backward)
    grad_hidden = jnp.where(order[tokens:].astype(F32) > 0, back_t[...].T, 0.0).astype(BF16)

    def gradient(i, carry):
        cols = chunk_of(i)
        value = jnp.dot(grad_hidden, w1v[:, cols], preferred_element_type=F32)
        grad_t[cols] = value.astype(BF16).T
        normed = (proj[:, cols].astype(F32) - centre) * inv_std
        scaled = value * gain[:, cols]
        both = scaled * normed
        sum1, sum2 = carry
        for k in range(CHUNK // LANES):
            lanes = slice(k * LANES, (k + 1) * LANES)
            sum1, sum2 = sum1 + scaled[:, lanes], sum2 + both[:, lanes]
        return sum1, sum2

    zero = jnp.zeros((tokens, LANES), F32)
    sum1, sum2 = lax.fori_loop(0, width // CHUNK, gradient, (zero, zero))
    square = (tokens, tokens)

    def as_row(column):
        return jnp.broadcast_to(column, square).T[0:1]

    mean1 = as_row(jnp.sum(sum1, axis=1, keepdims=True) / width)
    mean2 = as_row(jnp.sum(sum2, axis=1, keepdims=True) / width)
    row = lax.broadcasted_iota(jnp.int32, (PIECE, tokens), 0)
    tail = jnp.where(row == 0, mean1, jnp.where(row == 1, mean2, 0.0)).astype(BF16)
    stats[...] = jnp.where(row < 8, as_row(centre), as_row(inv_std))
    tile_rows = 2 * PIECE
    grad_rows = 8 * (size + PIECE)
    for i in range(8):

        def place_block(n, carry):
            base = pl.multiple_of(n * (size + PIECE), PIECE)
            outs[i][pl.ds(base, size)] = grad_t[block_of(i // 4, i % 4, n // 2, n % 2)]
            outs[i][pl.ds(base + size, PIECE)] = tail
            return carry

        lax.fori_loop(0, 8, place_block, 0, unroll=8)
    for i in range(8):
        base = 2 * i * PIECE
        hidden[base : base + PIECE] = order[i * PIECE : (i + 1) * PIECE]
        block = token_block(place, i)
        hidden[base + PIECE : base + 2 * PIECE] = order[at_piece(tokens // PIECE + block)]
    mine = at_piece(token_block(place, 0))

    def second(i, cols):
        value = jnp.dot(hidden[...], w2v[:, cols], preferred_element_type=F32)
        first_c = value[:PIECE] + own_rows(place, own_c[:, cols].astype(F32) + b2[:, cols])
        first_q = value[PIECE : 2 * PIECE] + own_rows(place, proj[mine, cols].astype(F32) + b2[:, cols])
        value = jnp.concatenate([first_c, first_q, value[2 * PIECE :]], axis=0).astype(BF16)
        tiles = CHUNK // LANES
        for k in range(8):
            base = grad_rows + i * tiles * tile_rows
            for j in range(tiles):
                spot = pl.ds(pl.multiple_of(base + j * tile_rows, tile_rows), tile_rows)
                outs[k][spot] = value[k * tile_rows : (k + 1) * tile_rows, j * LANES : (j + 1) * LANES]

    each_chunk(width, second)


def middle_kernel(place, *refs):
    sums, (own, *away), total = refs[:5], refs[6:10], refs[10]
    grad_rows = own.shape[1] // 14 * 5 * 8
    total[...] = sum(ref[grad_rows:].astype(F32) for ref in sums)
    ia, here = place[1], place[3]
    size = own.shape[1] // 14 * 5
    half = (own.shape[1] - size) // 2
    tile_rows = 2 * PIECE
    for j in range(4):
        out = own if j == 0 else away[j - 1]
        for other_x in range(2):
            a = lax.rem(ia - j + 4, 4)
            x = here + other_x - 2 * here * other_x
            spot = slice((j * 2 + other_x) * size, (j * 2 + other_x + 1) * size)
            out[other_x, :size] = sum(ref[spot].astype(F32) for ref in sums).astype(out.dtype)
            for kind in range(2):
                token = kind * PIECE + a * 4 + x * 2
                rows = [
                    total[pl.ds(token + r, half // 2, stride=tile_rows)] for r in range(2)
                ]
                base = size + kind * half
                out[other_x, base : base + half] = jnp.concatenate(rows, axis=0).astype(out.dtype)


ANY = pl.BlockSpec(memory_space=pl.ANY)
VMEM = pl.BlockSpec(memory_space=pltpu.VMEM)
SMEM = pl.BlockSpec(memory_space=pltpu.SMEM)


def call(kernel, ins, outs, scratch, limit, micros):
    return pl.pallas_call(
        kernel,
        in_specs=[spec for spec, _ in ins],
        out_specs=[spec for spec, _, _ in outs],
        out_shape=[jax.ShapeDtypeStruct(shape, dtype) for _, shape, dtype in outs],
        scratch_shapes=scratch,
        compiler_params=pltpu.CompilerParams(vmem_limit_bytes=limit * 1024 * 1024),
        cost_estimate=pl.CostEstimate(flops=0, bytes_accessed=micros * 3_690_000, transcendentals=0),
    )(*[value for _, value in ins])


def body(
    queries,
    w_proj,
    b_proj,
    captions,
    ln_gain,
    ln_bias,
    fc1_weight,
    fc1_bias,
    fc2_weight,
    fc2_bias,
    cotangent,
):
    where = lax.axis_index("fsdp")
    c = where % NC
    y = (where // NC) % NY
    z = (where // (NC * NY)) % NZ
    x = where // (NC * NY * NZ)
    ia = jnp.where(c == 0, z, y)
    ib = jnp.where(c == 0, y, z)
    place = jnp.stack([c, ia, ib, x, where]).astype(jnp.int32)
    rows, width = captions.shape
    qdim = queries.shape[1]
    cols = w_proj.shape[1]
    units = fc1_weight.shape[1]
    group = NX * NZ * NY * NC
    tokens = group * rows
    half = tokens // 2
    near = 8 * rows
    nw = rows * width // LANES

    def around(value, stage):
        return [value, *lax.optimization_barrier([send(value, ring_pairs(stage, k)) for k in (1, 2, 3)])]

    pack = jnp.concatenate([queries, captions, cotangent], axis=1)
    pack = gather2(pack, "x", x)
    pack = gather4(pack, STAGE_A, ia).reshape(near, -1)


    def both_cores(pieces):
        return pieces + [send(piece, swap_pairs("core")) for piece in pieces]

    pack_pieces = around(pack, STAGE_B)
    query_half = jnp.zeros((4, near, qdim), BF16)
    for k in range(4):
        query_half = put(query_half, pack_pieces[k][:, :qdim], (ib - k) % 4)
    query_all = gather2(query_half.reshape(half, qdim), "core", c).reshape(tokens, qdim)
    other_query = lax.ppermute(query_all, "dp", SENT)
    proj_own = (
        lax.dot_general(w_proj, query_all, (((0,), (1,)), ((), ())), preferred_element_type=F32)
        + b_proj.astype(F32)[:, None]
    ).astype(BF16)
    pack_pieces = both_cores(pack_pieces)

    pair = jnp.concatenate([proj_own, send(proj_own, swap_pairs("x"))], axis=0)
    pair, pack_pieces = lax.optimization_barrier((pair, pack_pieces))
    plane = jnp.concatenate(around(pair, STAGE_A), axis=0)
    proj_pieces = both_cores(around(plane, STAGE_B))
    scratch = pltpu.VMEM
    dma = pltpu.SemaphoreType.DMA

    gain, bias = ln_gain[None, :], ln_bias[None, :]
    b1, b2 = fc1_bias.astype(F32)[None, :], fc2_bias[None, :]
    w1_t = fc1_weight.T
    size = cols + PIECE

    act_c, cot, cot_own, own_c = call(
        early_kernel,
        [(SMEM, place)]
        + [(VMEM, piece) for piece in pack_pieces]
        + [(VMEM, gain), (VMEM, bias)],
        [(VMEM, (tokens, width), BF16)] * 2 + [(VMEM, (cols, tokens), F32), (VMEM, (PIECE, width), BF16)],
        [scratch((tokens, width), BF16), dma((16,))],
        16,
        5,
    )

    grad_rows, out_rows = 8 * size, width // LANES * 2 * PIECE
    piece_rows = grad_rows + out_rows
    *parts, stats = call(
        main_kernel,
        [(SMEM, place)]
        + [(VMEM, piece) for piece in proj_pieces]
        + [(VMEM, own_c), (VMEM, act_c), (VMEM, cot), (ANY, w1_t), (ANY, fc2_weight)]
        + [(VMEM, gain), (VMEM, bias), (VMEM, b1), (VMEM, b2)],
        [(VMEM, (piece_rows, LANES), BF16)] * 8 + [(VMEM, (PIECE, tokens), F32)],
        [
            scratch((width, tokens), BF16),
            scratch((tokens, width), BF16),
            scratch((units, 2 * tokens), F32),
            scratch((units, tokens), F32),
            scratch((2 * tokens, units), BF16),
            scratch((2 * tokens, units), BF16),
            scratch((units, width), BF16),
            scratch((units, width), BF16),
            dma((width // CHUNK,)),
            dma((width // CHUNK,)),
        ],
        36,
        20,
    )

    got = []
    for k in (2, 1, 3, 0):
        part = send(parts[4 + k], swap_pairs("core"))
        if k:
            part = (parts[k].astype(F32) + part.astype(F32)).astype(BF16)
            part = send(part, ring_pairs(STAGE_B, -k))
        got.append(part)
    last = size + 2 * nw
    own, *away = call(
        middle_kernel,
        [(SMEM, place)]
        + [(VMEM, part) for part in (parts[0], *got)]
        + [(ANY, other_query)],
        [(VMEM, (2, last, LANES), F32)] + [(VMEM, (2, last, LANES), BF16)] * 3,
        [scratch((out_rows, LANES), F32)],
        16,
        3,
    )
    got = lax.optimization_barrier([send(away[k - 1], ring_pairs(STAGE_A, -k)) for k in (1, 2, 3)])
    total = own + sum(part.astype(F32) for part in got)
    total = total[0] + send(total[1].astype(BF16), swap_pairs("x")).astype(F32)
    grad_act, mean1, mean2 = total[:cols], total[cols : cols + 1], total[cols + 1 : cols + 2]
    part = lax.optimization_barrier(total[size:].astype(BF16))
    out_captions, out_queries = part[:nw].reshape(rows, width), part[nw:].reshape(rows, width)

    gain_own = lax.dynamic_slice_in_dim(ln_gain, where * cols, cols, 0)[:, None]
    centre, inv_std = stats[0:1], stats[8:9]
    normed_own = (proj_own.astype(F32) - centre) * inv_std
    scaled = grad_act * gain_own
    grad_input = (cot_own + inv_std * (scaled - mean1 - normed_own * mean2)).astype(BF16)
    other_input = lax.ppermute(grad_input, "dp", SENT)

    def terms(query_rows, grads):
        weight = lax.dot_general(
            query_rows, grads, (((0,), (1,)), ((), ())), preferred_element_type=F32
        )
        return weight, jnp.sum(grads.astype(F32), axis=1)

    weight0, bias0 = terms(query_all, grad_input)
    weight1, bias1 = terms(other_query, other_input)
    return out_queries, out_captions, weight0 + weight1, bias0 + bias1


def solution(mesh):
    placed = (
        P(("fsdp", "dp"), None),
        P(None, "fsdp"),
        P("fsdp"),
        P(("fsdp", "dp"), None),
        P(),
        P(),
        P(None, "fsdp"),
        P("fsdp"),
        P("fsdp", None),
        P(),
        P(("fsdp", "dp"), None),
    )
    return jax.shard_map(
        body,
        mesh=mesh,
        in_specs=placed,
        out_specs=(P(("fsdp", "dp"), None), P(("fsdp", "dp"), None), P(None, "fsdp"), P("fsdp")),
        check_vma=False,
    )
```

```python
import jax
import jax.numpy as jnp
from jax import lax
from jax.experimental import pallas as pl
from jax.experimental.pallas import tpu as pltpu
from jax.sharding import PartitionSpec as P

F32 = jnp.float32
BF16 = jnp.bfloat16
NX, NZ, NY, NC = 2, 4, 4, 2
LANES = 128


def pos(x, z, y, c):
    return ((x * NZ + z) * NY + y) * NC + c


def ring_pairs(along_z, shift):
    pairs = []
    for x in range(NX):
        for z in range(NZ):
            for y in range(NY):
                for c in range(NC):
                    if along_z[c]:
                        to = pos(x, (z + shift) % NZ, y, c)
                    else:
                        to = pos(x, z, (y + shift) % NY, c)
                    pairs.append((pos(x, z, y, c), to))
    return pairs


def swap_pairs(axis):
    pairs = []
    for x in range(NX):
        for z in range(NZ):
            for y in range(NY):
                for c in range(NC):
                    to = pos(1 - x, z, y, c) if axis == "x" else pos(x, z, y, 1 - c)
                    pairs.append((pos(x, z, y, c), to))
    return pairs


STAGE_A = (True, False)
STAGE_B = (False, True)


def send(value, pairs):
    return lax.ppermute(value, "fsdp", pairs)


def put(buffer, piece, index):
    return lax.dynamic_update_slice_in_dim(buffer, piece[None], index, 0)


def gather2(shard, axis, index):
    buffer = jnp.zeros((2,) + shard.shape, shard.dtype)
    buffer = put(buffer, shard, index)
    return put(buffer, send(shard, swap_pairs(axis)), 1 - index)


def gather4(shard, stage, index):
    got = [send(shard, ring_pairs(stage, k)) for k in (1, 2, 3)]
    buffer = jnp.zeros((4,) + shard.shape, shard.dtype)
    buffer = put(buffer, shard, index)
    for k in (1, 2, 3):
        buffer = put(buffer, got[k - 1], (index - k) % 4)
    return buffer


def take(blocks, index):
    return lax.dynamic_index_in_dim(blocks, index, 0, keepdims=False)


def scatter2(blocks, axis, index):
    got = send(take(blocks, 1 - index), swap_pairs(axis))
    return take(blocks, index).astype(F32) + got.astype(F32)


def scatter4(blocks, stage, index):
    got = [send(take(blocks, (index + k) % 4), ring_pairs(stage, k)) for k in (1, 2, 3)]
    total = take(blocks, index).astype(F32)
    for piece in got:
        total = total + piece.astype(F32)
    return total


CHUNK = 3072
PIECE = 16
SENT = [(0, 1), (1, 0)]


def row_stats(ref, width):
    rows = ref.shape[0]
    step = width // 8

    def total(of):
        def add(i, acc):
            for j in range(step // LANES):
                acc = acc + of(ref[:, pl.ds(pl.multiple_of(i * step, LANES) + j * LANES, LANES)].astype(F32))
            return acc

        acc = lax.fori_loop(0, 8, add, jnp.zeros((rows, LANES), F32))
        return jnp.sum(acc, axis=1, keepdims=True) / width

    centre = total(lambda v: v)
    inv_std = 1.0 / jnp.sqrt(total(lambda v: (v - centre) * (v - centre)) + 1e-05)
    return centre, inv_std


def chunk_of(i):
    return pl.ds(pl.multiple_of(i * CHUNK, CHUNK), CHUNK)


def at_piece(i):
    return pl.ds(pl.multiple_of(i * PIECE, PIECE), PIECE)


def own_rows(place, value):
    first = (place[1] * 2 + place[3]) * 2
    row = lax.broadcasted_iota(jnp.int32, value.shape, 0)
    return jnp.where((row == first) | (row == first + 1), value, 0.0)


def columns_copy(source, target, sems, i):
    cols = chunk_of(i)
    return pltpu.make_async_copy(source.at[:, cols], target.at[:, cols], sems.at[i])


def each_chunk(width, step):
    def run(i, carry):
        step(i, chunk_of(i))
        return carry

    lax.fori_loop(0, width // CHUNK, run, 0)


def token_block(place, i):
    c, ia, ib = place[0], place[1], place[2]
    k = i % 4
    if i < 4:
        return c * 4 + lax.rem(ib - k + 4, 4)
    return (1 - c) * 4 + lax.rem(ia - k + 4, 4)


NT = (((1,), (1,)), ((), ()))


def early_kernel(place, *refs):
    pieces, refs = refs[:8], refs[8:]
    gain, bias, act, cot, cot_own, own, cap, sem = refs
    width = cap.shape[1]
    lead = pieces[0].shape[1] - 2 * width
    copies = []
    for i in range(8):
        near_rows = pieces[i].at[:, pl.ds(lead, width)]
        copies.append(pltpu.make_async_copy(near_rows, cap.at[pl.ds(i * PIECE, PIECE)], sem.at[i]))
    for copy in copies:
        copy.start()
    for i in range(8):
        near_rows = pieces[i].at[:, pl.ds(lead + width, width)]
        spot = at_piece(token_block(place, i))
        copies.append(pltpu.make_async_copy(near_rows, cot.at[spot], sem.at[8 + i]))
        copies[-1].start()
    for copy in copies[:8]:
        copy.wait()
    own[...] = cap[:PIECE]
    centre, inv_std = row_stats(cap, width)

    def step(i, cols):
        normed = (cap[:, cols].astype(F32) - centre) * inv_std
        act[:, cols] = (normed * gain[:, cols] + bias[:, cols]).astype(BF16)

    each_chunk(width, step)
    for copy in copies[8:]:
        copy.wait()
    size = cot_own.shape[0]
    start = place[4] * size
    aligned = pl.multiple_of(start // LANES * LANES, LANES)
    near = cot[:, pl.ds(aligned, 2 * LANES)].astype(F32)
    near = pltpu.roll(near, lax.rem(2 * LANES - lax.rem(start, LANES), 2 * LANES), 1)
    cot_own[...] = near.T[:size]


def main_kernel(place, *refs):
    pieces, refs = refs[:8], refs[8:]
    (own_c, act_c, cot, w1, w2, gain, bias, b1, b2), refs = refs[:9], refs[9:]
    outs, stats, refs = refs[:8], refs[8], refs[9:]
    proj_t, proj, acc, back_t, order, hidden, w1v, w2v, sem1, sem2 = refs
    grad_t = proj_t
    width = proj.shape[1]
    tokens = proj.shape[0]
    size = width // 64
    c, ia, ib = place[0], place[1], place[2]

    def block_of(half, k, j, other_x):
        if half == 0:
            core, a, b = c, lax.rem(ia - j + 4, 4), lax.rem(ib - k + 4, 4)
        else:
            core, a, b = 1 - c, lax.rem(ib - j + 4, 4), lax.rem(ia - k + 4, 4)
        x = place[3] + other_x - 2 * place[3] * other_x
        z_y = jnp.where(core == 0, a * 8 + b * 2, b * 8 + a * 2)
        return pl.ds(pl.multiple_of((x * 32 + z_y + core) * size, PIECE), size)

    each_chunk(width, lambda i, cols: columns_copy(w1, w1v, sem1, i).start())
    for i in range(8):

        def bring_block(n, carry):
            source = pl.ds(pl.multiple_of(n * size, PIECE), size)
            proj_t[block_of(i // 4, i % 4, n // 2, n % 2)] = pieces[i][source]
            return carry

        lax.fori_loop(0, 8, bring_block, 0, unroll=8)

    def turn(i, cols):
        proj[:, cols] = proj_t[cols].T

    each_chunk(width, turn)
    centre, inv_std = row_stats(proj, width)
    acc[...] = jnp.zeros_like(acc)

    def first(i, cols):
        normed = (proj[:, cols].astype(F32) - centre) * inv_std
        act = (normed * gain[:, cols] + bias[:, cols]).astype(BF16)
        act = jnp.concatenate([act_c[:, cols], act], axis=0)
        columns_copy(w1, w1v, sem1, i).wait()
        columns_copy(w2, w2v, sem2, i).start()
        acc[...] += lax.dot_general(w1v[:, cols], act, NT, preferred_element_type=F32)

    each_chunk(width, first)
    order[...] = jnp.maximum(acc[...].T + b1[...], 0.0).astype(BF16)
    back_t[...] = jnp.zeros_like(back_t)

    def backward(i, cols):
        columns_copy(w2, w2v, sem2, i).wait()
        back_t[...] += lax.dot_general(w2v[:, cols], cot[:, cols], NT, preferred_element_type=F32)

    each_chunk(width, backward)
    grad_hidden = jnp.where(order[tokens:].astype(F32) > 0, back_t[...].T, 0.0).astype(BF16)

    def gradient(i, carry):
        cols = chunk_of(i)
        value = jnp.dot(grad_hidden, w1v[:, cols], preferred_element_type=F32)
        grad_t[cols] = value.astype(BF16).T
        normed = (proj[:, cols].astype(F32) - centre) * inv_std
        scaled = value * gain[:, cols]
        both = scaled * normed
        sum1, sum2 = carry
        for k in range(CHUNK // LANES):
            lanes = slice(k * LANES, (k + 1) * LANES)
            sum1, sum2 = sum1 + scaled[:, lanes], sum2 + both[:, lanes]
        return sum1, sum2

    zero = jnp.zeros((tokens, LANES), F32)
    sum1, sum2 = lax.fori_loop(0, width // CHUNK, gradient, (zero, zero))
    square = (tokens, tokens)

    def as_row(column):
        return jnp.broadcast_to(column, square).T[0:1]

    mean1 = as_row(jnp.sum(sum1, axis=1, keepdims=True) / width)
    mean2 = as_row(jnp.sum(sum2, axis=1, keepdims=True) / width)
    row = lax.broadcasted_iota(jnp.int32, (PIECE, tokens), 0)
    tail = jnp.where(row == 0, mean1, jnp.where(row == 1, mean2, 0.0)).astype(BF16)
    stats[...] = jnp.where(row < 8, as_row(centre), as_row(inv_std))
    tile_rows = 2 * PIECE
    grad_rows = 8 * (size + PIECE)
    for i in range(8):

        def place_block(n, carry):
            base = pl.multiple_of(n * (size + PIECE), PIECE)
            outs[i][pl.ds(base, size)] = grad_t[block_of(i // 4, i % 4, n // 2, n % 2)]
            outs[i][pl.ds(base + size, PIECE)] = tail
            return carry

        lax.fori_loop(0, 8, place_block, 0, unroll=8)
    for i in range(8):
        base = 2 * i * PIECE
        hidden[base : base + PIECE] = order[i * PIECE : (i + 1) * PIECE]
        block = token_block(place, i)
        hidden[base + PIECE : base + 2 * PIECE] = order[at_piece(tokens // PIECE + block)]
    mine = at_piece(token_block(place, 0))

    def second(i, cols):
        value = jnp.dot(hidden[...], w2v[:, cols], preferred_element_type=F32)
        first_c = value[:PIECE] + own_rows(place, own_c[:, cols].astype(F32) + b2[:, cols])
        first_q = value[PIECE : 2 * PIECE] + own_rows(place, proj[mine, cols].astype(F32) + b2[:, cols])
        value = jnp.concatenate([first_c, first_q, value[2 * PIECE :]], axis=0).astype(BF16)
        tiles = CHUNK // LANES
        for k in range(8):
            base = grad_rows + i * tiles * tile_rows
            for j in range(tiles):
                spot = pl.ds(pl.multiple_of(base + j * tile_rows, tile_rows), tile_rows)
                outs[k][spot] = value[k * tile_rows : (k + 1) * tile_rows, j * LANES : (j + 1) * LANES]

    each_chunk(width, second)


def middle_kernel(place, *refs):
    sums, (own, *away), total = refs[:5], refs[6:10], refs[10]
    grad_rows = own.shape[1] // 14 * 5 * 8
    total[...] = sum(ref[grad_rows:].astype(F32) for ref in sums)
    ia, here = place[1], place[3]
    size = own.shape[1] // 14 * 5
    half = (own.shape[1] - size) // 2
    tile_rows = 2 * PIECE
    for j in range(4):
        out = own if j == 0 else away[j - 1]
        for other_x in range(2):
            a = lax.rem(ia - j + 4, 4)
            x = here + other_x - 2 * here * other_x
            spot = slice((j * 2 + other_x) * size, (j * 2 + other_x + 1) * size)
            out[other_x, :size] = sum(ref[spot].astype(F32) for ref in sums).astype(out.dtype)
            for kind in range(2):
                token = kind * PIECE + a * 4 + x * 2
                rows = [
                    total[pl.ds(token + r, half // 2, stride=tile_rows)] for r in range(2)
                ]
                base = size + kind * half
                out[other_x, base : base + half] = jnp.concatenate(rows, axis=0).astype(out.dtype)


ANY = pl.BlockSpec(memory_space=pl.ANY)
VMEM = pl.BlockSpec(memory_space=pltpu.VMEM)
SMEM = pl.BlockSpec(memory_space=pltpu.SMEM)


def call(kernel, ins, outs, scratch, limit, micros):
    return pl.pallas_call(
        kernel,
        in_specs=[spec for spec, _ in ins],
        out_specs=[spec for spec, _, _ in outs],
        out_shape=[jax.ShapeDtypeStruct(shape, dtype) for _, shape, dtype in outs],
        scratch_shapes=scratch,
        compiler_params=pltpu.CompilerParams(vmem_limit_bytes=limit * 1024 * 1024),
        cost_estimate=pl.CostEstimate(flops=0, bytes_accessed=micros * 3_690_000, transcendentals=0),
    )(*[value for _, value in ins])


def body(
    queries,
    w_proj,
    b_proj,
    captions,
    ln_gain,
    ln_bias,
    fc1_weight,
    fc1_bias,
    fc2_weight,
    fc2_bias,
    cotangent,
):
    where = lax.axis_index("fsdp")
    c = where % NC
    y = (where // NC) % NY
    z = (where // (NC * NY)) % NZ
    x = where // (NC * NY * NZ)
    ia = jnp.where(c == 0, z, y)
    ib = jnp.where(c == 0, y, z)
    place = jnp.stack([c, ia, ib, x, where]).astype(jnp.int32)
    rows, width = captions.shape
    qdim = queries.shape[1]
    cols = w_proj.shape[1]
    units = fc1_weight.shape[1]
    group = NX * NZ * NY * NC
    tokens = group * rows
    half = tokens // 2
    near = 8 * rows
    nw = rows * width // LANES

    def around(value, stage):
        two, one, three = lax.optimization_barrier([send(value, ring_pairs(stage, k)) for k in (2, 1, 3)])
        return [value, one, two, three]

    pack = jnp.concatenate([queries, captions, cotangent], axis=1)
    pack = gather2(pack, "x", x)
    pack = gather4(pack, STAGE_A, ia).reshape(near, -1)


    def both_cores(pieces):
        return pieces + [send(piece, swap_pairs("core")) for piece in pieces]

    pack_pieces = around(pack, STAGE_B)
    query_half = jnp.zeros((4, near, qdim), BF16)
    for k in range(4):
        query_half = put(query_half, pack_pieces[k][:, :qdim], (ib - k) % 4)
    query_all = gather2(query_half.reshape(half, qdim), "core", c).reshape(tokens, qdim)
    other_query = lax.ppermute(query_all, "dp", SENT)
    proj_own = (
        lax.dot_general(w_proj, query_all, (((0,), (1,)), ((), ())), preferred_element_type=F32)
        + b_proj.astype(F32)[:, None]
    ).astype(BF16)
    pack_pieces = both_cores(pack_pieces)

    pair = jnp.concatenate([proj_own, send(proj_own, swap_pairs("x"))], axis=0)
    pair, pack_pieces = lax.optimization_barrier((pair, pack_pieces))
    plane = jnp.concatenate(around(pair, STAGE_A), axis=0)
    proj_pieces = both_cores(around(plane, STAGE_B))
    scratch = pltpu.VMEM
    dma = pltpu.SemaphoreType.DMA

    gain, bias = ln_gain[None, :], ln_bias[None, :]
    b1, b2 = fc1_bias.astype(F32)[None, :], fc2_bias[None, :]
    w1_t = fc1_weight.T
    size = cols + PIECE

    act_c, cot, cot_own, own_c = call(
        early_kernel,
        [(SMEM, place)]
        + [(VMEM, piece) for piece in pack_pieces]
        + [(VMEM, gain), (VMEM, bias)],
        [(VMEM, (tokens, width), BF16)] * 2 + [(VMEM, (cols, tokens), F32), (VMEM, (PIECE, width), BF16)],
        [scratch((tokens, width), BF16), dma((16,))],
        16,
        5,
    )

    grad_rows, out_rows = 8 * size, width // LANES * 2 * PIECE
    piece_rows = grad_rows + out_rows
    *parts, stats = call(
        main_kernel,
        [(SMEM, place)]
        + [(VMEM, piece) for piece in proj_pieces]
        + [(VMEM, own_c), (VMEM, act_c), (VMEM, cot), (ANY, w1_t), (ANY, fc2_weight)]
        + [(VMEM, gain), (VMEM, bias), (VMEM, b1), (VMEM, b2)],
        [(VMEM, (piece_rows, LANES), BF16)] * 8 + [(VMEM, (PIECE, tokens), F32)],
        [
            scratch((width, tokens), BF16),
            scratch((tokens, width), BF16),
            scratch((units, 2 * tokens), F32),
            scratch((units, tokens), F32),
            scratch((2 * tokens, units), BF16),
            scratch((2 * tokens, units), BF16),
            scratch((units, width), BF16),
            scratch((units, width), BF16),
            dma((width // CHUNK,)),
            dma((width // CHUNK,)),
        ],
        36,
        20,
    )

    got = []
    for k in (1, 3, 2, 0):
        part = send(parts[4 + k], swap_pairs("core"))
        if k:
            part = (parts[k].astype(F32) + part.astype(F32)).astype(BF16)
            part = send(part, ring_pairs(STAGE_B, -k))
        got.append(part)
    last = size + 2 * nw
    own, *away = call(
        middle_kernel,
        [(SMEM, place)]
        + [(VMEM, part) for part in (parts[0], *got)]
        + [(ANY, other_query)],
        [(VMEM, (2, last, LANES), F32)] + [(VMEM, (2, last, LANES), BF16)] * 3,
        [scratch((out_rows, LANES), F32)],
        16,
        3,
    )
    got = lax.optimization_barrier([send(away[k - 1], ring_pairs(STAGE_A, -k)) for k in (1, 2, 3)])
    total = own + sum(part.astype(F32) for part in got)
    total = total[0] + send(total[1].astype(BF16), swap_pairs("x")).astype(F32)
    grad_act, mean1, mean2 = total[:cols], total[cols : cols + 1], total[cols + 1 : cols + 2]
    part = lax.optimization_barrier(total[size:].astype(BF16))
    out_captions, out_queries = part[:nw].reshape(rows, width), part[nw:].reshape(rows, width)

    gain_own = lax.dynamic_slice_in_dim(ln_gain, where * cols, cols, 0)[:, None]
    centre, inv_std = stats[0:1], stats[8:9]
    normed_own = (proj_own.astype(F32) - centre) * inv_std
    scaled = grad_act * gain_own
    grad_input = (cot_own + inv_std * (scaled - mean1 - normed_own * mean2)).astype(BF16)
    other_input = lax.ppermute(grad_input, "dp", SENT)

    def terms(query_rows, grads):
        weight = lax.dot_general(
            query_rows, grads, (((0,), (1,)), ((), ())), preferred_element_type=F32
        )
        return weight, jnp.sum(grads.astype(F32), axis=1)

    weight0, bias0 = terms(query_all, grad_input)
    weight1, bias1 = terms(other_query, other_input)
    return out_queries, out_captions, weight0 + weight1, bias0 + bias1


def solution(mesh):
    placed = (
        P(("fsdp", "dp"), None),
        P(None, "fsdp"),
        P("fsdp"),
        P(("fsdp", "dp"), None),
        P(),
        P(),
        P(None, "fsdp"),
        P("fsdp"),
        P("fsdp", None),
        P(),
        P(("fsdp", "dp"), None),
    )
    return jax.shard_map(
        body,
        mesh=mesh,
        in_specs=placed,
        out_specs=(P(("fsdp", "dp"), None), P(("fsdp", "dp"), None), P(None, "fsdp"), P("fsdp")),
        check_vma=False,
    )
```
